32 devices in a mesh: tm: 4 (over x, core), vocab: 8 (over z, y).
Axes of the slice: x: 2, y: 2, z: 4, core: 2. Of those that a mesh axis runs over, the one named last changes fastest.
Arguments:
- frames: bfloat16 [768, 1024], P(('tm', 'vocab')), may hold values from -6 to 6
- qkv_weight: bfloat16 [1024, 3072], replicated, may hold values from -0.375 to 0.375
- attn_out_weight: bfloat16 [1024, 1024], replicated, may hold values from -0.1875 to 0.1875
- head_weight: bfloat16 [1024, 16384], P('tm', 'vocab'), may hold values from -0.5 to 0.5
- back_weight: bfloat16 [16384, 1024], P('vocab', 'tm'), may hold values from -6 to 6
Outputs:
- conditioned: bfloat16 [768, 1024], P(('tm', 'vocab'))
- log_norm: float32 [768], P(('tm', 'vocab'))
The draws below stay inside these ranges and needn't reach their ends.
All inputs are finite; a program needn't handle non-finite values.
Results may differ from the reference program's by a relative error of at most 0.017.
The reference program's roundings to bfloat16 on the way (of `normed`, `project`, `weights`, `context`, `hidden`, `unit` and `label_probs`) count: a program that leaves them out, or rounds other values in their place, can miss the bound.
Values may be sent and summed in bfloat16 or wider, within the bound.
A program may use at most 128 MiB of HBM per device.

```python
import math
import jax
import jax.numpy as jnp
from jax import lax

D = 1024
HEADS = 16
HEAD_DIM = 64
WIN = 128
FR_DEV = 24
VOCAB = 16384
TOKENS = 768
N_VOCAB = 8


def draw_qkv_weight(key, part):
    base_draw = jnp.clip(jax.random.normal(key, (D, 3 * D), jnp.float32), -4.0, 4.0)
    column_index = jnp.arange(3 * D, dtype=jnp.int32)
    column_scale = jnp.where(column_index < 2 * D, 3.0, 1.0) / math.sqrt(D)
    return (base_draw * column_scale[None, :]).astype(jnp.bfloat16)


def level_of(own_key, shape, shards, low, high):
    def one(dim, parts):
        steps = jax.random.uniform(jax.random.fold_in(jax.random.fold_in(own_key, 6), dim), (parts,), jnp.float32, low / len(shards), high / len(shards))
        return jnp.repeat(jnp.exp(steps), shape[dim] // parts).reshape((-1,) + (1,) * (len(shape) - dim - 1))

    level = one(*shards[0])
    for cut in shards[1:]:
        level = level * one(*cut)
    return level


def bell_draw(stream_key, shape, scale, reach, shards=(), kind=jnp.bfloat16):
    values = scale * jax.random.normal(stream_key, shape, jnp.float32)
    if shards:
        values = values * level_of(stream_key, shape, shards, -0.22, 0.18)
    return jnp.clip(values, -reach, reach).astype(kind)


def setup_inputs(seed: int = 0) -> dict:
    keys = jax.random.split(jax.random.key(seed), 6)
    return {
        "frames": bell_draw(keys[0], (TOKENS, D), 1.0, 6.0, ((0, 32),)),
        "qkv_weight": draw_qkv_weight(jax.random.fold_in(keys[5], 71), 0),
        "attn_out_weight": bell_draw(keys[2], (D, D), D ** -0.5, 0.1875),
        "head_weight": bell_draw(keys[3], (D, VOCAB), (D // 9) ** -0.5, 0.5, ((0, 4), (1, 8))),
        "back_weight": bell_draw(keys[4], (VOCAB, D), 1.0, 6.0, ((0, 8), (1, 4))),
    }


def root_norm(values):
    return values * lax.rsqrt(lax.optimization_barrier(jnp.mean(values * values, axis=-1, keepdims=True)) + 1e-06)

def reference(frames, qkv_weight, attn_out_weight, head_weight, back_weight):
    total_frames = frames.shape[0]
    model_width = frames.shape[1]
    normed = root_norm(frames.astype(jnp.float32)).astype(jnp.bfloat16)
    project = jnp.dot(normed, qkv_weight, preferred_element_type=jnp.float32).astype(jnp.bfloat16)
    query = project[:, :model_width].reshape(total_frames, HEADS, HEAD_DIM)
    padded = jnp.concatenate([jnp.zeros((WIN, 2 * model_width), jnp.bfloat16), project[:, model_width:]], axis=0)

    def attend(block_id):
        first = block_id * WIN
        query_blk = lax.dynamic_slice_in_dim(query, first, WIN, 0).astype(jnp.float32)
        pair_blk = lax.dynamic_slice_in_dim(padded, first, 2 * WIN, 0)
        key_blk = pair_blk[:, :model_width].reshape(2 * WIN, HEADS, HEAD_DIM).astype(jnp.float32)
        value_blk = pair_blk[:, model_width:].reshape(2 * WIN, HEADS, HEAD_DIM).astype(jnp.float32)
        scores = jnp.einsum('qhd,khd->hqk', query_blk, key_blk) / math.sqrt(HEAD_DIM)
        scores = 50.0 * jnp.tanh(scores / 50.0)
        query_pos = first + jnp.arange(WIN, dtype=jnp.int32)
        key_pos = first - WIN + jnp.arange(2 * WIN, dtype=jnp.int32)
        allowed = (key_pos[None, :] <= query_pos[:, None]) & (key_pos[None, :] > query_pos[:, None] - WIN) & (key_pos[None, :] >= 0)
        expo = jnp.where(allowed[None], jnp.exp(scores), 0.0)
        weights = (expo / lax.optimization_barrier(jnp.sum(expo, axis=-1, keepdims=True))).astype(jnp.bfloat16)
        context = jnp.einsum('hqk,khd->qhd', weights.astype(jnp.float32), value_blk)
        return context.astype(jnp.bfloat16).reshape(WIN, model_width)
    context = lax.map(attend, jnp.arange(total_frames // WIN, dtype=jnp.int32)).reshape(total_frames, model_width)
    hidden = (frames.astype(jnp.float32) + jnp.dot(context, attn_out_weight, preferred_element_type=jnp.float32)).astype(jnp.bfloat16)
    unit = root_norm(hidden.astype(jnp.float32)).astype(jnp.bfloat16)
    group = FR_DEV * N_VOCAB

    def head_block(block_id):
        rows_blk = lax.dynamic_slice_in_dim(unit, block_id * group, group, 0)
        logits = jnp.dot(rows_blk, head_weight, preferred_element_type=jnp.float32)
        logits = 30.0 * jnp.tanh(logits / 30.0)
        label_probs = jnp.exp(logits).astype(jnp.bfloat16)
        totals = lax.optimization_barrier(jnp.sum(label_probs.astype(jnp.float32), axis=-1))
        partial_value = jnp.dot(label_probs, back_weight, preferred_element_type=jnp.float32)
        return (partial_value / totals[:, None], jnp.log(totals))
    back_proj, log_norm = lax.map(head_block, jnp.arange(total_frames // group, dtype=jnp.int32))
    back_proj = back_proj.reshape(total_frames, model_width)
    log_norm = log_norm.reshape(total_frames)
    center = back_proj - lax.optimization_barrier(jnp.mean(back_proj, axis=-1, keepdims=True))
    spread = lax.optimization_barrier(jnp.mean(center * center, axis=-1, keepdims=True))
    conditioned = (hidden.astype(jnp.float32) + center * lax.rsqrt(spread + 1e-05)).astype(jnp.bfloat16)
    return (conditioned, log_norm)
```

```python
import functools
import math

import jax
import jax.numpy as jnp
from jax import lax
from jax.experimental import pallas as pl
from jax.experimental.pallas import tpu as pltpu
from jax.sharding import PartitionSpec as P

HEADS = 16
HEAD_DIM = 64
WIN = 128
LANES = 128
BF16 = jnp.bfloat16
F32 = jnp.float32
MESH = pl.DeviceIdType.MESH


def root_norm(values):
    return values * lax.rsqrt(jnp.mean(values * values, axis=-1, keepdims=True) + 1e-06)


def pack(main, tot):
    lane = lax.broadcasted_iota(jnp.int32, (main.shape[0], LANES), 1)
    high = tot.astype(BF16).astype(F32)
    tail = jnp.where(lane == 0, high, jnp.where(lane == 1, tot - high, 0.0))
    return jnp.concatenate([main, tail], axis=1).astype(BF16)


def unpack(packed, width):
    wide = packed.astype(F32)
    return wide[:, :width], jnp.sum(wide[:, width:], axis=-1, keepdims=True)


def kernel(
    n_tm, n_voc, rows, width, hops, group,
    frames_ref, qkv_ref, out_ref, head_ref, back_ref,
    cond_ref, log_ref,
    fr, wq, wo, head, back, units, parts, near, sums, far, owned,
    loc_sem, halo_s, halo_r, head_s, head_r, back_s, back_r,
    voc_s, voc_r, sib_s, sib_r, far_s, far_r, near_s, near_r, sum_s, sum_r, own_s, own_r,
):
    t = lax.axis_index("tm")
    v = lax.axis_index("vocab")
    n_dev = n_tm * n_voc
    pairs = n_tm // 2
    me = t * n_voc + v
    sib = t + 1 - 2 * lax.rem(t, 2)
    depth = head_ref.shape[0]
    labels = head.shape[1]
    chunks = n_voc // group

    def remote(src, dst, ss, rs, dev):
        return pltpu.make_async_remote_copy(
            src_ref=src, dst_ref=dst, send_sem=ss, recv_sem=rs, device_id=dev, device_id_type=MESH
        )

    def other(k):
        return lax.rem(t + k, n_tm)

    def linear(i):
        return (i // n_voc, lax.rem(i, n_voc))

    def head_rows(i):
        return head.at[pl.ds(pl.multiple_of(i * depth, depth), depth)]

    def back_cols(i):
        return back.at[:, pl.ds(pl.multiple_of(i * depth, depth), depth)]

    def head_part(i):
        return head_ref.at[:, pl.ds(pl.multiple_of(i * labels, labels), labels)]

    def back_part(i):
        return back_ref.at[pl.ds(pl.multiple_of(i * labels, labels), labels)]

    local = [
        pltpu.make_async_copy(frames_ref, fr.at[hops], loc_sem.at[0]),
        pltpu.make_async_copy(qkv_ref, wq, loc_sem.at[1]),
        pltpu.make_async_copy(out_ref, wo, loc_sem.at[2]),
        pltpu.make_async_copy(head_part(t), head_rows(t), loc_sem.at[3]),
        pltpu.make_async_copy(back_part(t), back_cols(t), loc_sem.at[4]),
    ]
    for copy in local:
        copy.start()

    barrier = pltpu.get_barrier_semaphore()
    greet = lambda dev: pl.semaphore_signal(barrier, inc=1, device_id=dev, device_id_type=MESH)
    for k in range(1, n_tm):
        greet((other(k), v))
    lax.fori_loop(1, n_voc, lambda k, c: (greet((t, lax.rem(v + k, n_voc))), c)[1], 0)
    for s in range(1, hops + 1):
        @pl.when(me + s < n_dev)
        def _():
            greet(linear(me + s))

        @pl.when(me >= s)
        def _():
            greet(linear(me - s))

    pl.semaphore_wait(
        barrier,
        n_tm - 1 + n_voc - 1 + jnp.minimum(hops, me) + jnp.minimum(hops, n_dev - 1 - me),
    )

    def halo(s):
        return remote(frames_ref, fr.at[hops - s], halo_s.at[s - 1], halo_r.at[s - 1], linear(me + s))

    for s in range(1, hops + 1):
        @pl.when(me + s < n_dev)
        def _():
            halo(s).start()

        @pl.when(me < s)
        def _():
            fr[hops - s] = jnp.zeros((rows, width), BF16)

    order = [k for k in range(2, n_tm)] + [1]
    head_copies, back_copies = [], []
    for k in order:
        p = other(k)
        head_copies.append(remote(head_part(p), head_rows(t), head_s.at[k - 1], head_r.at[k - 1], (p, v)))
        back_copies.append(remote(back_part(p), back_cols(t), back_s.at[k - 1], back_r.at[k - 1], (p, v)))
    for copy in head_copies + back_copies:
        copy.start()

    local[0].wait()
    for s in range(1, hops + 1):
        @pl.when(me >= s)
        def _():
            remote(frames_ref, fr.at[hops - s], halo_s.at[s - 1], halo_r.at[s - 1], (t, v)).wait_recv()

    own = fr[hops].astype(F32)
    blocks = [fr[i].astype(F32) for i in range(hops)] + [own]
    used = (hops + 1) * rows
    keys = (used + LANES - 1) // LANES * LANES
    if keys > used:
        blocks.append(jnp.zeros((keys - used, width), F32))
    normed = root_norm(jnp.concatenate(blocks, axis=0)).astype(BF16)
    query_in = root_norm(own).astype(BF16)
    local[1].wait()
    local[2].wait()
    query = jnp.dot(query_in, wq[:, :width], preferred_element_type=F32)
    key_part = jnp.dot(normed, wq[:, width : 2 * width], preferred_element_type=F32).astype(BF16)
    value_part = jnp.dot(normed, wq[:, 2 * width :], preferred_element_type=F32).astype(BF16)
    per = LANES // HEAD_DIM
    row = lax.broadcasted_iota(jnp.int32, (rows, keys), 0)
    col = lax.broadcasted_iota(jnp.int32, (rows, keys), 1)
    gap = row + hops * rows - col
    allowed = (gap >= 0) & (gap < WIN) & (col + (me - hops) * rows >= 0)
    allowed = jnp.concatenate([allowed.astype(F32)] * per, axis=0) > 0.5
    lane = lax.broadcasted_iota(jnp.int32, (rows, LANES), 1)
    context = []
    for g in range(width // LANES):
        cols = slice(g * LANES, (g + 1) * LANES)
        q = query[:, cols]
        stacked = jnp.concatenate(
            [jnp.where(lane // HEAD_DIM == h, q, 0.0) for h in range(per)], axis=0
        ).astype(BF16)
        scores = lax.dot_general(
            stacked, key_part[:, cols], (((1,), (1,)), ((), ())), preferred_element_type=F32
        ) / math.sqrt(HEAD_DIM)
        scores = 50.0 * jnp.tanh(scores / 50.0)
        expo = jnp.where(allowed, jnp.exp(scores), 0.0)
        weights = (expo / jnp.sum(expo, axis=-1, keepdims=True)).astype(BF16)
        ctx = jnp.dot(weights, value_part[:, cols], preferred_element_type=F32)
        mixed = ctx[:rows]
        for h in range(1, per):
            mixed = jnp.where(lane // HEAD_DIM == h, ctx[h * rows : (h + 1) * rows], mixed)
        context.append(mixed)
    context = jnp.concatenate(context, axis=1).astype(BF16)
    hidden = (own + jnp.dot(context, wo[...], preferred_element_type=F32)).astype(BF16).astype(F32)
    units[t, v] = root_norm(hidden).astype(BF16)

    def voc_copy(k):
        w = lax.rem(v + k, n_voc)
        return remote(units.at[t, v], units.at[t, v], voc_s.at[k - 1], voc_r.at[k - 1], (t, w))

    def far_copy(a, w):
        return remote(
            units.at[t, w], units.at[t, w], far_s.at[a - 1, w], far_r.at[a - 1, w], (other(2 * a), v)
        )

    def sib_copy(a, w):
        o = other(2 * a)
        return remote(units.at[o, w], units.at[o, w], sib_s.at[a, w], sib_r.at[a, w], (sib, v))

    def pass_on(w):
        for a in range(1, pairs):
            far_copy(a, w).start()
        sib_copy(0, w).start()

    def loop(lo, hi, fn):
        def step(i, c):
            fn(i)
            return c

        lax.fori_loop(lo, hi, step, 0)

    loop(1, n_voc, lambda k: voc_copy(k).start())
    pass_on(v)

    def voc_arrived(k):
        voc_copy(k).wait_recv()
        pass_on(lax.rem(v + n_voc - k, n_voc))

    loop(1, n_voc, voc_arrived)

    def process(block):
        def chunk(c):
            u = jnp.concatenate(
                [units[block, c * group + j].astype(F32) for j in range(group)], axis=0
            ).astype(BF16)
            logits = jnp.dot(u, head[...], preferred_element_type=F32)
            probs = jnp.exp(30.0 * jnp.tanh(logits / 30.0)).astype(BF16)
            tot = jnp.sum(probs.astype(F32), axis=-1, keepdims=True)
            packed = pack(jnp.dot(probs, back[...], preferred_element_type=F32), tot).astype(F32)
            for j in range(group):
                parts[block, c * group + j] = packed[j * rows : (j + 1) * rows].astype(BF16)

        loop(0, chunks, chunk)

    def near_copy(a):
        return remote(parts.at[lax.rem(sib + 2 * a, n_tm)], near.at[a], near_s.at[a], near_r.at[a], (sib, v))

    local[3].wait()
    for copy in head_copies:
        copy.wait_recv()
    local[4].wait()
    for copy in back_copies:
        copy.wait_recv()
    process(t)
    for a in range(1, pairs):
        def far_arrived(k):
            w = lax.rem(v + n_voc - k, n_voc)
            far_copy(pairs - a, w).wait_recv()
            sib_copy(a, w).start()

        loop(0, n_voc, far_arrived)
    for a in range(pairs):
        if a:
            process(other(2 * a))
        loop(0, n_voc, lambda k: sib_copy(a, lax.rem(v + n_voc - k, n_voc)).wait_recv())
        process(lax.rem(sib + 2 * a, n_tm))
        near_copy(a).start()

    def sum_copy(a, w):
        return remote(
            sums.at[a - 1, w], far.at[a - 1, w], sum_s.at[a - 1, w], sum_r.at[a - 1, w], (other(2 * a), v)
        )

    for a in range(1, pairs):
        near_copy(a).wait_recv()

        def pair_sum(k):
            w = lax.rem(v + k, n_voc)
            m0, t0 = unpack(parts[other(2 * a), w], width)
            m1, t1 = unpack(near[a, w], width)
            sums[a - 1, w] = pack(m0 + m1, t0 + t1)
            sum_copy(a, w).start()

        loop(1, n_voc + 1, pair_sum)
    near_copy(0).wait_recv()

    def own_copy(k):
        w = lax.rem(v + k, n_voc)
        return remote(parts.at[t, w], owned.at[k - 1], own_s.at[k - 1], own_r.at[k - 1], (t, w))

    def tm_sum(w):
        m, s = unpack(parts[t, w], width)
        m1, s1 = unpack(near[0, w], width)
        m, s = m + m1, s + s1
        for a in range(1, pairs):
            sum_copy(a, w).wait_recv()
            m1, s1 = unpack(far[a - 1, w], width)
            m, s = m + m1, s + s1
        return m, s

    def send_sum(k):
        w = lax.rem(v + k, n_voc)
        m, s = tm_sum(w)
        parts[t, w] = pack(m, s)
        own_copy(k).start()

    loop(1, n_voc, send_sum)
    total, tot = tm_sum(v)
    for k in range(1, n_voc):
        own_copy(k).wait_recv()
        m1, s1 = unpack(owned[k - 1], width)
        total, tot = total + m1, tot + s1
    value = total / tot
    center = value - jnp.mean(value, axis=-1, keepdims=True)
    spread = jnp.mean(center * center, axis=-1, keepdims=True)
    cond_ref[...] = (hidden + center * lax.rsqrt(spread + 1e-05)).astype(BF16)
    r = lax.broadcasted_iota(jnp.int32, (rows, LANES), 0)
    c = lax.broadcasted_iota(jnp.int32, (rows, LANES), 1)
    log_ref[...] = jnp.sum(jnp.where(r == c, jnp.log(tot), 0.0), axis=0, keepdims=True)

    for s in range(1, hops + 1):
        @pl.when(me + s < n_dev)
        def _():
            halo(s).wait_send()
    for copy in head_copies + back_copies:
        copy.wait_send()
    loop(1, n_voc, lambda k: voc_copy(k).wait_send())
    loop(1, n_voc, lambda k: own_copy(k).wait_send())

    def rest(w):
        for a in range(pairs):
            sib_copy(a, w).wait_send()
            if a:
                far_copy(a, w).wait_send()
                sum_copy(a, w).wait_send()

    loop(0, n_voc, rest)
    for a in range(pairs):
        near_copy(a).wait_send()


def body(n_tm, n_voc, frames, qkv_weight, attn_out_weight, head_weight, back_weight):
    rows, width = frames.shape
    hops = (WIN + rows - 1) // rows
    labels = head_weight.shape[1] // n_tm
    pairs = n_tm // 2
    group = max(1, min(n_voc, 192 // rows))
    while n_voc % group:
        group -= 1
    wide = width + LANES
    far_count = max(1, pairs - 1)
    dma = pltpu.SemaphoreType.DMA
    conditioned, logs = pl.pallas_call(
        functools.partial(kernel, n_tm, n_voc, rows, width, hops, group),
        out_shape=(
            jax.ShapeDtypeStruct((rows, width), BF16),
            jax.ShapeDtypeStruct((1, LANES), F32),
        ),
        in_specs=[pl.BlockSpec(memory_space=pl.ANY)] * 5,
        out_specs=(pl.BlockSpec(memory_space=pltpu.VMEM),) * 2,
        scratch_shapes=[
            pltpu.VMEM((hops + 1, rows, width), BF16),
            pltpu.VMEM(qkv_weight.shape, BF16),
            pltpu.VMEM(attn_out_weight.shape, BF16),
            pltpu.VMEM((width, labels), BF16),
            pltpu.VMEM((labels, width), BF16),
            pltpu.VMEM((n_tm, n_voc, rows, width), BF16),
            pltpu.VMEM((n_tm, n_voc, rows, wide), BF16),
            pltpu.VMEM((pairs, n_voc, rows, wide), BF16),
            pltpu.VMEM((far_count, n_voc, rows, wide), BF16),
            pltpu.VMEM((far_count, n_voc, rows, wide), BF16),
            pltpu.VMEM((n_voc - 1, rows, wide), BF16),
            dma((5,)),
            dma((hops,)), dma((hops,)),
            dma((n_tm - 1,)), dma((n_tm - 1,)),
            dma((n_tm - 1,)), dma((n_tm - 1,)),
            dma((n_voc - 1,)), dma((n_voc - 1,)),
            dma((pairs, n_voc)), dma((pairs, n_voc)),
            dma((far_count, n_voc)), dma((far_count, n_voc)),
            dma((pairs,)), dma((pairs,)),
            dma((far_count, n_voc)), dma((far_count, n_voc)),
            dma((n_voc - 1,)), dma((n_voc - 1,)),
        ],
        compiler_params=pltpu.CompilerParams(
            collective_id=0, has_side_effects=True, vmem_limit_bytes=63 * 1024 * 1024
        ),
    )(frames, qkv_weight, attn_out_weight, head_weight, back_weight)
    return conditioned, logs[0, :rows]


def solution(mesh):
    return jax.shard_map(
        functools.partial(body, mesh.shape["tm"], mesh.shape["vocab"]),
        mesh=mesh,
        in_specs=(P(("tm", "vocab"), None), P(), P(), P("tm", "vocab"), P("vocab", "tm")),
        out_specs=(P(("tm", "vocab"), None), P(("tm", "vocab"))),
        check_vma=False,
    )
```

```python
import functools
import math

import jax
import jax.numpy as jnp
from jax import lax
from jax.experimental import pallas as pl
from jax.experimental.pallas import tpu as pltpu
from jax.sharding import PartitionSpec as P

HEADS = 16
HEAD_DIM = 64
WIN = 128
LANES = 128
BF16 = jnp.bfloat16
F32 = jnp.float32
MESH = pl.DeviceIdType.MESH


def root_norm(values):
    return values * lax.rsqrt(jnp.mean(values * values, axis=-1, keepdims=True) + 1e-06)


def pack(main, tot):
    lane = lax.broadcasted_iota(jnp.int32, (main.shape[0], LANES), 1)
    high = tot.astype(BF16).astype(F32)
    tail = jnp.where(lane == 0, high, jnp.where(lane == 1, tot - high, 0.0))
    return jnp.concatenate([main, tail], axis=1).astype(BF16)


def unpack(packed, width):
    wide = packed.astype(F32)
    return wide[:, :width], jnp.sum(wide[:, width:], axis=-1, keepdims=True)


def kernel(
    n_tm, n_voc, rows, width, hops, group,
    frames_ref, qkv_ref, out_ref, head_ref, back_ref,
    cond_ref, log_ref,
    fr, wq, wo, head, back, units, parts, near, sums, far, owned, across,
    loc_sem, swap_s, swap_r, halo_s, halo_r, head_s, head_r, back_s, back_r,
    voc_s, voc_r, fwd_s, fwd_r, sib_s, sib_r, near_s, near_r, sum_s, sum_r, acr_s, acr_r, own_s, own_r,
):
    t = lax.axis_index("tm")
    v = lax.axis_index("vocab")
    n_dev = n_tm * n_voc
    pairs = n_tm // 2
    me = t * n_voc + v
    sib = t + 1 - 2 * lax.rem(t, 2)
    depth = head_ref.shape[0]
    labels = head.shape[1]
    chunks = n_voc // group
    half = n_voc // 2
    side = lax.rem(v, 2)
    mate = v + 1 - 2 * side
    lane_pos = v // 2

    def remote(src, dst, ss, rs, dev):
        return pltpu.make_async_remote_copy(
            src_ref=src, dst_ref=dst, send_sem=ss, recv_sem=rs, device_id=dev, device_id_type=MESH
        )

    def other(k):
        return lax.rem(t + k, n_tm)

    def linear(i):
        return (i // n_voc, lax.rem(i, n_voc))

    def head_rows(i):
        return head.at[pl.ds(pl.multiple_of(i * depth, depth), depth)]

    def back_cols(i):
        return back.at[:, pl.ds(pl.multiple_of(i * depth, depth), depth)]

    def head_part(i):
        return head_ref.at[:, pl.ds(pl.multiple_of(i * labels, labels), labels)]

    def back_part(i):
        return back_ref.at[pl.ds(pl.multiple_of(i * labels, labels), labels)]

    local = [
        pltpu.make_async_copy(frames_ref, fr.at[0, hops], loc_sem.at[0]),
        pltpu.make_async_copy(qkv_ref, wq, loc_sem.at[1]),
        pltpu.make_async_copy(out_ref, wo, loc_sem.at[2]),
        pltpu.make_async_copy(head_part(t), head_rows(t), loc_sem.at[3]),
        pltpu.make_async_copy(back_part(t), back_cols(t), loc_sem.at[4]),
    ]
    for copy in local:
        copy.start()

    barrier = pltpu.get_barrier_semaphore()
    greet = lambda dev: pl.semaphore_signal(barrier, inc=1, device_id=dev, device_id_type=MESH)
    for k in range(1, n_tm):
        greet((other(k), v))
    lax.fori_loop(1, n_voc, lambda k, c: (greet((t, lax.rem(v + k, n_voc))), c)[1], 0)
    for s in range(1, hops + 1):
        greet(linear(lax.rem(me + s, n_dev)))
        greet(linear(lax.rem(me + n_dev - s, n_dev)))
    pl.semaphore_wait(barrier, n_tm - 1 + n_voc - 1 + 2 * hops)

    place = [lax.rem(me + 2 * a * n_voc, n_dev) for a in range(pairs)]

    def halo(a, s):
        src = fr.at[a, hops] if a else frames_ref
        return remote(
            src, fr.at[a, hops - s], halo_s.at[a, s - 1], halo_r.at[a, s - 1],
            linear(lax.rem(me + s, n_dev)),
        )

    def start_halo(a):
        for s in range(1, hops + 1):
            @pl.when(place[a] + s < n_dev)
            def _():
                halo(a, s).start()

            @pl.when(place[a] < s)
            def _():
                fr[a, hops - s] = jnp.zeros((rows, width), BF16)

    swaps = [
        remote(frames_ref, fr.at[pairs - a, hops], swap_s.at[pairs - a - 1], swap_r.at[pairs - a - 1], (other(2 * a), v))
        for a in range(1, pairs)
    ]
    for copy in swaps:
        copy.start()
    start_halo(0)

    order = [k for k in range(2, n_tm)] + [1]
    head_copies, back_copies = [], []
    for k in order:
        p = other(k)
        head_copies.append(remote(head_part(p), head_rows(t), head_s.at[k - 1], head_r.at[k - 1], (p, v)))
        back_copies.append(remote(back_part(p), back_cols(t), back_s.at[k - 1], back_r.at[k - 1], (p, v)))
    for copy in head_copies:
        copy.start()
    for copy in swaps:
        copy.wait_recv()
    for a in range(1, pairs):
        start_halo(a)
    for copy in back_copies:
        copy.start()

    local[0].wait()
    used = (hops + 1) * rows
    keys = (used + LANES - 1) // LANES * LANES
    per = LANES // HEAD_DIM
    row = lax.broadcasted_iota(jnp.int32, (rows, keys), 0)
    col = lax.broadcasted_iota(jnp.int32, (rows, keys), 1)
    gap = row + hops * rows - col
    lane = lax.broadcasted_iota(jnp.int32, (rows, LANES), 1)
    local[1].wait()
    local[2].wait()

    def attend(a):
        for s in range(1, hops + 1):
            @pl.when(place[a] >= s)
            def _():
                halo(a, s).wait_recv()

        own = fr[a, hops].astype(F32)
        blocks = [fr[a, i].astype(F32) for i in range(hops)] + [own]
        if keys > used:
            blocks.append(jnp.zeros((keys - used, width), F32))
        normed = root_norm(jnp.concatenate(blocks, axis=0)).astype(BF16)
        query_in = root_norm(own).astype(BF16)
        query = jnp.dot(query_in, wq[:, :width], preferred_element_type=F32)
        key_part = jnp.dot(normed, wq[:, width : 2 * width], preferred_element_type=F32).astype(BF16)
        value_part = jnp.dot(normed, wq[:, 2 * width :], preferred_element_type=F32).astype(BF16)
        allowed = (gap >= 0) & (gap < WIN) & (col + (place[a] - hops) * rows >= 0)
        allowed = jnp.concatenate([allowed.astype(F32)] * per, axis=0) > 0.5
        context = []
        for g in range(width // LANES):
            cols = slice(g * LANES, (g + 1) * LANES)
            q = query[:, cols]
            stacked = jnp.concatenate(
                [jnp.where(lane // HEAD_DIM == h, q, 0.0) for h in range(per)], axis=0
            ).astype(BF16)
            scores = lax.dot_general(
                stacked, key_part[:, cols], (((1,), (1,)), ((), ())), preferred_element_type=F32
            ) / math.sqrt(HEAD_DIM)
            scores = 50.0 * jnp.tanh(scores / 50.0)
            expo = jnp.where(allowed, jnp.exp(scores), 0.0)
            weights = (expo / jnp.sum(expo, axis=-1, keepdims=True)).astype(BF16)
            ctx = jnp.dot(weights, value_part[:, cols], preferred_element_type=F32)
            mixed = ctx[:rows]
            for h in range(1, per):
                mixed = jnp.where(lane // HEAD_DIM == h, ctx[h * rows : (h + 1) * rows], mixed)
            context.append(mixed)
        context = jnp.concatenate(context, axis=1).astype(BF16)
        out = (own + jnp.dot(context, wo[...], preferred_element_type=F32)).astype(BF16).astype(F32)
        units[other(2 * a), v] = root_norm(out).astype(BF16)
        return out

    def spot(k):
        return 2 * lax.rem(lane_pos + k, half) + side

    def voc_copy(a, k):
        o = other(2 * a)
        w = mate if k is None else spot(k)
        i = 0 if k is None else k
        return remote(units.at[o, v], units.at[o, v], voc_s.at[a, i], voc_r.at[a, i], (t, w))

    def fwd_copy(a, k):
        o, w = other(2 * a), spot(half - k)
        return remote(units.at[o, w], units.at[o, w], fwd_s.at[a, k - 1], fwd_r.at[a, k - 1], (t, mate))

    def sib_copy(a, w):
        o = other(2 * a)
        return remote(units.at[o, w], units.at[o, w], sib_s.at[a, w], sib_r.at[a, w], (sib, v))

    def loop(lo, hi, fn):
        def step(i, c):
            fn(i)
            return c

        lax.fori_loop(lo, hi, step, 0)

    def push(a):
        loop(1, half, lambda k: voc_copy(a, k).start())
        voc_copy(a, None).start()
        sib_copy(a, v).start()

    hidden = attend(0)
    push(0)
    for a in range(1, pairs):
        attend(a)
        push(a)
    for a in range(pairs):
        voc_copy(a, None).wait_recv()
        sib_copy(a, mate).start()

        def side_arrived(k):
            voc_copy(a, k).wait_recv()
            fwd_copy(a, k).start()
            sib_copy(a, spot(half - k)).start()

        loop(1, half, side_arrived)

        def mate_arrived(k):
            fwd_copy(a, k).wait_recv()
            sib_copy(a, spot(half - k) + 1 - 2 * side).start()

        loop(1, half, mate_arrived)

    def process(block):
        def chunk(c):
            u = jnp.concatenate(
                [units[block, c * group + j].astype(F32) for j in range(group)], axis=0
            ).astype(BF16)
            logits = jnp.dot(u, head[...], preferred_element_type=F32)
            probs = jnp.exp(30.0 * jnp.tanh(logits / 30.0)).astype(BF16)
            tot = jnp.sum(probs.astype(F32), axis=-1, keepdims=True)
            packed = pack(jnp.dot(probs, back[...], preferred_element_type=F32), tot).astype(F32)
            for j in range(group):
                parts[block, c * group + j] = packed[j * rows : (j + 1) * rows].astype(BF16)

        loop(0, chunks, chunk)

    def near_copy(a):
        return remote(parts.at[lax.rem(sib + 2 * a, n_tm)], near.at[a], near_s.at[a], near_r.at[a], (sib, v))

    local[3].wait()
    for copy in head_copies:
        copy.wait_recv()
    local[4].wait()
    for copy in back_copies:
        copy.wait_recv()
    for a in [*range(1, pairs), 0]:
        process(other(2 * a))
        loop(0, n_voc, lambda w: sib_copy(a, w).wait_recv())
        process(lax.rem(sib + 2 * a, n_tm))
        near_copy(a).start()

    def sum_copy(a, w):
        return remote(
            sums.at[a - 1, w], far.at[a - 1, w], sum_s.at[a - 1, w], sum_r.at[a - 1, w], (other(2 * a), v)
        )

    for a in range(1, pairs):
        near_copy(a).wait_recv()

        def pair_sum(k):
            w = 2 * lax.rem(lane_pos + k // 2, half) + lax.rem(side + 1 + k, 2)
            m0, t0 = unpack(parts[other(2 * a), w], width)
            m1, t1 = unpack(near[a, w], width)
            sums[a - 1, w] = pack(m0 + m1, t0 + t1)
            sum_copy(a, w).start()

        loop(2, n_voc + 2, pair_sum)
    near_copy(0).wait_recv()

    def across_copy(k):
        w = spot(k) + 1 - 2 * side
        return remote(parts.at[t, w], across.at[k - 1], acr_s.at[k - 1], acr_r.at[k - 1], (t, mate))

    def own_copy(k):
        w = spot(k)
        return remote(parts.at[t, w], owned.at[k - 1], own_s.at[k - 1], own_r.at[k - 1], (t, w))

    def tm_sum(w):
        m, s = unpack(parts[t, w], width)
        m1, s1 = unpack(near[0, w], width)
        m, s = m + m1, s + s1
        for a in range(1, pairs):
            sum_copy(a, w).wait_recv()
            m1, s1 = unpack(far[a - 1, w], width)
            m, s = m + m1, s + s1
        return m, s

    def send_across(k):
        w = spot(k) + 1 - 2 * side
        m, s = tm_sum(w)
        parts[t, w] = pack(m, s)
        across_copy(k).start()

    def both_sides(k):
        m, s = tm_sum(spot(k))
        across_copy(k).wait_recv()
        m1, s1 = unpack(across[k - 1], width)
        return m + m1, s + s1

    def send_sum(k):
        send_across(k)
        m, s = both_sides(k)
        parts[t, spot(k)] = pack(m, s)
        own_copy(k).start()

    loop(1, half, send_sum)
    send_across(half)
    total, tot = both_sides(half)
    for k in range(1, half):
        own_copy(k).wait_recv()
        m1, s1 = unpack(owned[k - 1], width)
        total, tot = total + m1, tot + s1
    value = total / tot
    center = value - jnp.mean(value, axis=-1, keepdims=True)
    spread = jnp.mean(center * center, axis=-1, keepdims=True)
    cond_ref[...] = (hidden + center * lax.rsqrt(spread + 1e-05)).astype(BF16)
    r = lax.broadcasted_iota(jnp.int32, (rows, LANES), 0)
    c = lax.broadcasted_iota(jnp.int32, (rows, LANES), 1)
    log_ref[...] = jnp.sum(jnp.where(r == c, jnp.log(tot), 0.0), axis=0, keepdims=True)

    for a in range(pairs):
        for s in range(1, hops + 1):
            @pl.when(place[a] + s < n_dev)
            def _():
                halo(a, s).wait_send()
        voc_copy(a, None).wait_send()

        def sent(k):
            voc_copy(a, k).wait_send()
            fwd_copy(a, k).wait_send()

        loop(1, half, sent)
    for copy in swaps + head_copies + back_copies:
        copy.wait_send()
    loop(1, half, lambda k: own_copy(k).wait_send())
    loop(1, half + 1, lambda k: across_copy(k).wait_send())

    def rest(w):
        for a in range(pairs):
            sib_copy(a, w).wait_send()
            if a:
                sum_copy(a, w).wait_send()

    loop(0, n_voc, rest)
    for a in range(pairs):
        near_copy(a).wait_send()


def body(n_tm, n_voc, frames, qkv_weight, attn_out_weight, head_weight, back_weight):
    rows, width = frames.shape
    hops = (WIN + rows - 1) // rows
    labels = head_weight.shape[1] // n_tm
    pairs = n_tm // 2
    half = n_voc // 2
    group = max(1, min(n_voc, 192 // rows))
    while n_voc % group:
        group -= 1
    wide = width + LANES
    far_count = max(1, pairs - 1)
    dma = pltpu.SemaphoreType.DMA
    conditioned, logs = pl.pallas_call(
        functools.partial(kernel, n_tm, n_voc, rows, width, hops, group),
        out_shape=(
            jax.ShapeDtypeStruct((rows, width), BF16),
            jax.ShapeDtypeStruct((1, LANES), F32),
        ),
        in_specs=[pl.BlockSpec(memory_space=pl.ANY)] * 5,
        out_specs=(pl.BlockSpec(memory_space=pltpu.VMEM),) * 2,
        scratch_shapes=[
            pltpu.VMEM((pairs, hops + 1, rows, width), BF16),
            pltpu.VMEM(qkv_weight.shape, BF16),
            pltpu.VMEM(attn_out_weight.shape, BF16),
            pltpu.VMEM((width, labels), BF16),
            pltpu.VMEM((labels, width), BF16),
            pltpu.VMEM((n_tm, n_voc, rows, width), BF16),
            pltpu.VMEM((n_tm, n_voc, rows, wide), BF16),
            pltpu.VMEM((pairs, n_voc, rows, wide), BF16),
            pltpu.VMEM((far_count, n_voc, rows, wide), BF16),
            pltpu.VMEM((far_count, n_voc, rows, wide), BF16),
            pltpu.VMEM((half, rows, wide), BF16),
            pltpu.VMEM((half, rows, wide), BF16),
            dma((5,)),
            dma((far_count,)), dma((far_count,)),
            dma((pairs, hops)), dma((pairs, hops)),
            dma((n_tm - 1,)), dma((n_tm - 1,)),
            dma((n_tm - 1,)), dma((n_tm - 1,)),
            dma((pairs, half)), dma((pairs, half)),
            dma((pairs, half)), dma((pairs, half)),
            dma((pairs, n_voc)), dma((pairs, n_voc)),
            dma((pairs,)), dma((pairs,)),
            dma((far_count, n_voc)), dma((far_count, n_voc)),
            dma((half,)), dma((half,)),
            dma((half,)), dma((half,)),
        ],
        compiler_params=pltpu.CompilerParams(
            collective_id=0, has_side_effects=True, vmem_limit_bytes=63 * 1024 * 1024
        ),
    )(frames, qkv_weight, attn_out_weight, head_weight, back_weight)
    return conditioned, logs[0, :rows]


def solution(mesh):
    return jax.shard_map(
        functools.partial(body, mesh.shape["tm"], mesh.shape["vocab"]),
        mesh=mesh,
        in_specs=(P(("tm", "vocab"), None), P(), P(), P("tm", "vocab"), P("vocab", "tm")),
        out_specs=(P(("tm", "vocab"), None), P(("tm", "vocab"))),
        check_vma=False,
    )
```
